32 devices in a mesh: ex: 4 (over y, core), proj: 8 (over z, x).
Axes of the slice: x: 2, y: 2, z: 4, core: 2. Of those that a mesh axis runs over, the one named last changes fastest.
Arguments:
- queries: bfloat16 [1024, 65536], P('ex', 'proj'), as said below
- train_grads: bfloat16 [2048, 65536], P('ex', 'proj'), as said below
- query_weight: float32 [1024], P('proj'), may hold values from 0.3 to 3
Outputs:
- scores: bfloat16 [1024, 2048], P('proj', 'ex')
- influence: float32 [2048], P('ex')
The draws below stay inside these ranges and needn't reach their ends.
Inputs may be any that keep to these rules, and one draw needn't show every extreme that they name: `queries`: finite real gradient entries. `train_grads`: finite real gradient entries.
All inputs are finite; a program needn't handle non-finite values.
Results may differ from the reference program's by a relative error of at most 0.00055.
Values may be sent and summed in bfloat16 or wider, within the bound.
A program may use at most 128 MiB of HBM per device.

```python
import math
import jax
import jax.numpy as jnp
from jax import lax

P_SIZE = 8192
LAYERS = 8
NQ = 1024
NT = 2048


def grad_field(key, rows, cols):
    keys = jax.random.split(key, 5)
    normal_part = jax.random.normal(keys[0], (rows, cols), jnp.float32)
    base = normal_part
    row_scale = jnp.exp(jax.random.uniform(keys[3], (rows, 1), jnp.float32) * math.log(10.0))
    rising = jnp.exp(math.log(3.0) * jnp.arange(cols, dtype=jnp.float32) / cols)[None, :]
    col_scale = jnp.exp(jax.random.uniform(keys[4], (1, cols), jnp.float32) * math.log(4.0)) * rising
    return base * row_scale * col_scale


def draw_queries(key, part):
    key = jax.random.fold_in(key, 11)
    return grad_field(key, NQ, LAYERS * P_SIZE).astype(jnp.bfloat16)


def draw_train_grads(key, part):
    key = jax.random.fold_in(key, 23)
    return grad_field(key, NT, LAYERS * P_SIZE).astype(jnp.bfloat16)


def block_scale(stream_key, shape, pieces, smallest, largest):
    gain, own = 1.0, jax.random.fold_in(stream_key, 6)
    for dim, blocks in pieces:
        steps = jnp.exp(jax.random.uniform(jax.random.fold_in(own, dim), (blocks,), jnp.float32, smallest / len(pieces), largest / len(pieces)))
        gain = gain * jnp.repeat(steps, shape[dim] // blocks).reshape([-1 if axis == dim else 1 for axis in range(len(shape))])
    return gain


def setup_inputs(seed: int = 0) -> dict:
    splits = jax.random.split(jax.random.key(seed), 4)
    return {
        "queries": draw_queries(jax.random.fold_in(splits[3], 71), 0),
        "train_grads": draw_train_grads(jax.random.fold_in(splits[3], 71), 0),
        "query_weight": jnp.clip(jnp.exp(math.log(3.0) - 2.3025851 * jax.random.uniform(splits[2], (NQ,), jnp.float32) ** block_scale(splits[2], (NQ,), ((0, 8),), -0.2, 0.2)), 0.3, 3.0),
    }


def reference(queries, train_grads, query_weight):
    qf = queries.astype(jnp.float32)
    tf = train_grads.astype(jnp.float32)
    query_sq = lax.optimization_barrier(jnp.sum(qf * qf, axis=1))
    train_sq = lax.optimization_barrier(jnp.sum(tf * tf, axis=1))
    dots = lax.dot_general(queries, train_grads, (((1,), (1,)), ((), ())), preferred_element_type=jnp.float32)
    scaled = (LAYERS * P_SIZE) ** 0.5 * dots * lax.rsqrt(query_sq + 1e-06)[:, None] * lax.rsqrt(train_sq + 1e-06)[None, :]
    scores = scaled.astype(jnp.bfloat16)
    influence = jnp.dot(query_weight, scaled, precision=lax.Precision.HIGHEST) * NQ ** (-0.5)
    return (scores, influence)
```

```python
import functools

import jax
import jax.numpy as jnp
from jax import lax
from jax.experimental import pallas as pl
from jax.experimental.pallas import tpu as pltpu
from jax.sharding import PartitionSpec as P

MESH = pl.DeviceIdType.MESH
SLAB = 16
AHEAD = 2
LANES = 128


def kernel(
    ex, proj, q_hbm, t_hbm, w_ref,
    scores_ref, infl_ref,
    qbuf, tbuf, part, rs_buf, tacc, t_own, t_buf, i_own, i_buf, scaled_ref,
    load_sem, y_send, y_recv, sib_send, sib_recv, rs_send, rs_recv, t_send, t_recv, i_send, i_recv,
):
    nb, rows_p, cols = q_hbm.shape
    n = t_hbm.shape[0]
    chips = ex // 2
    chunks = rows_p // SLAB
    group = 2 * nb
    e = lax.axis_index("ex")
    p = lax.axis_index("proj")
    y, core = e // 2, e % 2
    sibling = e + 1 - 2 * core

    load_t = pltpu.make_async_copy(t_hbm, tbuf, load_sem.at[0])
    load_q = pltpu.make_async_copy(q_hbm, qbuf.at[pl.ds(e * nb, nb)], load_sem.at[1])

    barrier = pltpu.get_barrier_semaphore()
    for d in range(1, chips):
        pl.semaphore_signal(barrier, inc=1, device_id={"ex": lax.rem(y + d, chips) * 2 + core}, device_id_type=MESH)
    pl.semaphore_signal(barrier, inc=1, device_id={"ex": sibling}, device_id_type=MESH)
    for d in range(1, proj):
        pl.semaphore_signal(barrier, inc=1, device_id={"proj": lax.rem(p + d, proj)}, device_id_type=MESH)
    load_t.start()
    load_q.start()
    pl.semaphore_wait(barrier, chips + proj - 1)

    def rows_of(c):
        return pl.ds(pl.multiple_of(c * SLAB, SLAB), SLAB)

    def send_y(i):
        d, c = i // chunks, lax.rem(i, chunks)
        pltpu.make_async_remote_copy(
            src_ref=q_hbm.at[:, rows_of(c)],
            dst_ref=qbuf.at[pl.ds(e * nb, nb), rows_of(c)],
            send_sem=y_send.at[d],
            recv_sem=y_recv.at[d, c],
            device_id={"ex": lax.rem(y + d + 1, chips) * 2 + core},
            device_id_type=MESH,
        ).start()

    def sib_copy(s, c, own):
        at = (lax.rem(y - s + chips, chips) * 2 + core) * nb
        dst = qbuf.at[pl.ds(at, nb), rows_of(c)]
        return pltpu.make_async_remote_copy(
            src_ref=q_hbm.at[:, rows_of(c)] if own else dst,
            dst_ref=dst,
            send_sem=sib_send.at[s],
            recv_sem=sib_recv.at[s, c],
            device_id={"ex": sibling},
            device_id_type=MESH,
        )

    total = (chips - 1) * chunks
    for i in range(min(AHEAD, total)):
        send_y(jnp.int32(i))
    for c in range(chunks):
        sib_copy(0, c, True).start()

    load_t.wait()

    def t_rows(g, carry):
        rows = pl.ds(pl.multiple_of(g * SLAB, SLAB), SLAB)
        acc = jnp.zeros((SLAB, LANES), jnp.float32)
        for k in range(0, cols, LANES):
            x = tbuf[rows, k : k + LANES].astype(jnp.float32)
            acc = acc + x * x
        tacc[rows, :] = acc
        return carry

    lax.fori_loop(0, n // SLAB, t_rows, 0)
    t_own[...] = jnp.sum(tacc[...].T.reshape(LANES // 8, 8, n), axis=0)

    def to_all(src, buf, send, recv):
        for d in range(1, proj):
            pltpu.make_async_remote_copy(
                src_ref=src,
                dst_ref=buf.at[d - 1],
                send_sem=send.at[0],
                recv_sem=recv.at[0],
                device_id={"proj": lax.rem(p + d, proj)},
                device_id_type=MESH,
            ).start()

    def wait_for(ref, sem):
        pltpu.make_async_copy(ref, ref, sem).wait()

    to_all(t_own, t_buf, t_send, t_recv)
    load_q.wait()

    def finish(c):
        rows = rows_of(c)
        wait_for(rs_buf.at[:, rows], rs_recv.at[c])
        tot = part[p, rows, :]
        for j in range(proj - 1):
            tot = tot + rs_buf[j, rows, :]
        query_sq = jnp.sum(tot[:, n:], axis=1, keepdims=True)
        scaled = (
            float(cols * proj) ** 0.5
            * tot[:, :n]
            * lax.rsqrt(query_sq + 1e-06)
            * lax.rsqrt(t_own[0:1, :] + 1e-06)
        )
        scaled_ref[rows, :] = scaled
        scores_ref[rows, :] = scaled.astype(jnp.bfloat16)

    def step(i, carry):
        s, c = i // chunks, lax.rem(i, chunks)
        late = i - chunks
        chip = lax.rem(y - s + chips, chips)

        @pl.when(s > 0)
        def _():
            got = qbuf.at[pl.ds((chip * 2 + core) * nb, nb), rows_of(c)]
            wait_for(got, y_recv.at[s - 1, c])
            sib_copy(s, c, False).start()

            @pl.when(late + AHEAD < total)
            def _():
                send_y(late + AHEAD)

        wait_for(qbuf.at[pl.ds((chip * 2 + 1 - core) * nb, nb), rows_of(c)], sib_recv.at[s, c])
        blocks = pl.ds(chip * group, group)
        depth = min(cols, 2048)
        acc = jnp.zeros((group * SLAB, n), jnp.float32)
        for k in range(0, cols, depth):
            x = qbuf[blocks, rows_of(c), k : k + depth].reshape(group * SLAB, depth)
            acc = acc + lax.dot_general(
                x, tbuf[:, k : k + depth], (((1,), (1,)), ((), ())), preferred_element_type=jnp.float32
            )
        part[blocks, rows_of(c), :n] = acc.reshape(group, SLAB, n)
        sq = jnp.zeros((group, SLAB, LANES), jnp.float32)
        for k in range(0, cols, LANES):
            x = qbuf[blocks, rows_of(c), k : k + LANES].astype(jnp.float32)
            sq = sq + x * x
        part[blocks, rows_of(c), n:] = sq
        for b in range(group):
            to = chip * group + b

            @pl.when(to != p)
            def _():
                pltpu.make_async_remote_copy(
                    src_ref=part.at[to, rows_of(c)],
                    dst_ref=rs_buf.at[lax.rem(to - p + proj, proj) - 1, rows_of(c)],
                    send_sem=rs_send.at[0],
                    recv_sem=rs_recv.at[c],
                    device_id={"proj": to},
                    device_id_type=MESH,
                ).start()

        @pl.when(i == chunks * chips - chunks)
        def _():
            wait_for(t_buf, t_send.at[0])
            wait_for(t_buf, t_recv.at[0])
            tot = t_own[...]
            for j in range(proj - 1):
                tot = tot + t_buf[j]
            t_own[...] = jnp.broadcast_to(jnp.sum(tot, axis=0, keepdims=True), tot.shape)

        @pl.when(i > chunks * chips - chunks)
        def _():
            finish(c - 1)

        return carry

    lax.fori_loop(0, chips * chunks, step, 0)
    finish(jnp.int32(chunks - 1))

    weighted = jnp.dot(
        jnp.broadcast_to(w_ref[...], (8, rows_p)),
        scaled_ref[...],
        precision=lax.Precision.HIGHEST,
        preferred_element_type=jnp.float32,
    )
    i_own[...] = weighted
    to_all(i_own, i_buf, i_send, i_recv)
    for s in range(chips):
        wait_for(q_hbm, sib_send.at[s])
    for d in range(chips - 1):
        wait_for(q_hbm, y_send.at[d])
    wait_for(rs_buf, rs_send.at[0])
    wait_for(i_buf, i_recv.at[0])
    tot = weighted
    for j in range(proj - 1):
        tot = tot + i_buf[j]
    infl_ref[...] = tot[0:1, :] * (proj * rows_p) ** (-0.5)
    wait_for(i_buf, i_send.at[0])


def body(ex, proj, queries, train_grads, query_weight):
    rows, cols = queries.shape
    n = train_grads.shape[0]
    rows_p = query_weight.shape[0]
    nb = rows // rows_p
    chips, chunks = ex // 2, rows_p // SLAB
    width = n + LANES
    f32, bf16 = jnp.float32, jnp.bfloat16
    vmem = pl.BlockSpec(memory_space=pltpu.VMEM)
    anywhere = pl.BlockSpec(memory_space=pl.ANY)
    dma = pltpu.SemaphoreType.DMA
    scores, influence = pl.pallas_call(
        functools.partial(kernel, ex, proj),
        out_shape=(jax.ShapeDtypeStruct((rows_p, n), bf16), jax.ShapeDtypeStruct((1, n), f32)),
        in_specs=[anywhere, anywhere, vmem],
        out_specs=(vmem, vmem),
        scratch_shapes=[
            pltpu.VMEM((proj, rows_p, cols), bf16),
            pltpu.VMEM((n, cols), bf16),
            pltpu.VMEM((proj, rows_p, width), f32),
            pltpu.VMEM((proj - 1, rows_p, width), f32),
            pltpu.VMEM((n, LANES), f32),
            pltpu.VMEM((8, n), f32),
            pltpu.VMEM((proj - 1, 8, n), f32),
            pltpu.VMEM((8, n), f32),
            pltpu.VMEM((proj - 1, 8, n), f32),
            pltpu.VMEM((rows_p, n), f32),
            dma((2,)),
            dma((chips - 1,)),
            dma((chips - 1, chunks)),
            dma((chips,)),
            dma((chips, chunks)),
            dma((1,)),
            dma((chunks,)),
            dma((1,)),
            dma((1,)),
            dma((1,)),
            dma((1,)),
        ],
        compiler_params=pltpu.CompilerParams(
            collective_id=0, has_side_effects=True, vmem_limit_bytes=56 * 2**20
        ),
        name="scores_ring",
    )(queries.reshape(nb, rows_p, cols), train_grads, query_weight.reshape(1, rows_p))
    return scores, influence.reshape(n)


def solution(mesh):
    return jax.shard_map(
        functools.partial(body, mesh.shape["ex"], mesh.shape["proj"]),
        mesh=mesh,
        in_specs=(P("ex", "proj"), P("ex", "proj"), P("proj")),
        out_specs=(P("proj", "ex"), P("ex")),
        check_vma=False,
    )
```

```python
import functools

import jax
import jax.numpy as jnp
from jax import lax
from jax.experimental import pallas as pl
from jax.experimental.pallas import tpu as pltpu
from jax.sharding import PartitionSpec as P

MESH = pl.DeviceIdType.MESH
SLAB = 16
FIRST = 2
LANES = 128
PROMPT = 3


def kernel(
    ex, proj, q_hbm, t_hbm, w_ref,
    scores_ref, infl_ref,
    qbuf, tbuf, part, pair_buf, rs_buf, lanes, m_own, m_buf, w_buf, q_rows, q_col, wq_col, t_scale, v_own, v_buf,
    load_sem, y_send, y_recv, sib_send, sib_recv, pair_send, pair_recv, rs_send, rs_recv,
    m_send, m_recv, w_send, w_recv, n_send, n_recv, v_send, v_recv,
):
    nb, rows_p, cols = q_hbm.shape
    n = t_hbm.shape[0]
    rows_e = nb * rows_p
    chips = ex // 2
    half = proj // 2
    chunks = rows_p // SLAB
    group = 2 * nb
    e = lax.axis_index("ex")
    p = lax.axis_index("proj")
    y, core = e // 2, e % 2
    z, x = p // 2, p % 2
    sibling = e + 1 - 2 * core
    partner = p + 1 - 2 * x

    load_t = pltpu.make_async_copy(t_hbm, tbuf, load_sem.at[0])
    load_q = pltpu.make_async_copy(q_hbm, qbuf.at[pl.ds(e * nb, nb)], load_sem.at[1])

    barrier = pltpu.get_barrier_semaphore()
    for d in range(1, ex):
        pl.semaphore_signal(barrier, inc=1, device_id={"ex": lax.rem(e + d, ex)}, device_id_type=MESH)
    for d in range(1, proj):
        pl.semaphore_signal(barrier, inc=1, device_id={"proj": lax.rem(p + d, proj)}, device_id_type=MESH)
    load_q.start()
    load_t.start()
    pl.semaphore_wait(barrier, ex + proj - 2)

    def rows_of(c):
        return pl.ds(pl.multiple_of(c * SLAB, SLAB), SLAB)

    def send_y(i):
        d, c = i // chunks, lax.rem(i, chunks)
        pltpu.make_async_remote_copy(
            src_ref=q_hbm.at[:, rows_of(c)],
            dst_ref=qbuf.at[pl.ds(e * nb, nb), rows_of(c)],
            send_sem=y_send.at[d],
            recv_sem=y_recv.at[d, c],
            device_id={"ex": lax.rem(y + d + 1, chips) * 2 + core},
            device_id_type=MESH,
        ).start()

    def sib_copy(s, c, own):
        at = (lax.rem(y - s + chips, chips) * 2 + core) * nb
        dst = qbuf.at[pl.ds(at, nb), rows_of(c)]
        return pltpu.make_async_remote_copy(
            src_ref=q_hbm.at[:, rows_of(c)] if own else dst,
            dst_ref=dst,
            send_sem=sib_send.at[s],
            recv_sem=sib_recv.at[s, c],
            device_id={"ex": sibling},
            device_id_type=MESH,
        )

    total = (chips - 1) * chunks
    for i in range(min(FIRST, total)):
        send_y(jnp.int32(i))

    def to_all(src, slot, send, recv):
        for d in range(1, proj):
            pltpu.make_async_remote_copy(
                src_ref=src,
                dst_ref=slot(d),
                send_sem=send.at[0],
                recv_sem=recv.at[0],
                device_id={"proj": lax.rem(p + d, proj)},
                device_id_type=MESH,
            ).start()

    def wait_for(ref, sem):
        pltpu.make_async_copy(ref, ref, sem).wait()

    w_buf[0] = jnp.broadcast_to(w_ref[...], (8, rows_p))
    to_all(w_buf.at[0], lambda d: w_buf.at[d], w_send, w_recv)
    for c in range(chunks):
        sib_copy(0, c, True).start()

    def norms(count, at, load):
        def one(g, carry):
            acc = jnp.zeros((SLAB, LANES), jnp.float32)
            for k in range(0, cols, LANES):
                v = load(g, k).astype(jnp.float32)
                acc = acc + v * v
            lanes[pl.ds(pl.multiple_of(at + g * SLAB, SLAB), SLAB), :] = acc
            return carry

        lax.fori_loop(0, count // SLAB, one, 0)

    load_q.wait()
    norms(rows_e, n, lambda g, k: qbuf[e * nb + g // chunks, rows_of(lax.rem(g, chunks)), k : k + LANES])
    load_t.wait()
    norms(n, 0, lambda g, k: tbuf[rows_of(g), k : k + LANES])
    m_own[...] = jnp.sum(lanes[...].T.reshape(LANES // 8, 8, n + rows_e), axis=0)
    to_all(m_own, lambda d: m_buf.at[d - 1], m_send, m_recv)
    wait_for(m_buf, m_recv.at[0])
    tot = m_own[...]
    for j in range(proj - 1):
        tot = tot + m_buf[j]
    tot = jnp.broadcast_to(jnp.sum(tot, axis=0, keepdims=True), tot.shape)
    scale = lax.rsqrt(tot + 1e-06)
    t_scale[...] = scale[:, :n]
    q_rows[0] = scale[:, n:]
    for d in range(1, ex):
        pltpu.make_async_remote_copy(
            src_ref=q_rows.at[0],
            dst_ref=q_rows.at[d],
            send_sem=n_send.at[0],
            recv_sem=n_recv.at[jnp.where(lax.rem(e + d, ex) == sibling, 0, 1)],
            device_id={"ex": lax.rem(e + d, ex)},
            device_id_type=MESH,
        ).start()
    for i in range(min(FIRST, total), total):
        send_y(jnp.int32(i))
    wait_for(w_buf.at[pl.ds(1, proj - 1)], w_recv.at[0])
    for d in range(proj):
        row = jnp.broadcast_to(w_buf[d, 0:1, :], (LANES, rows_p))
        wq_col[lax.rem(p - d + proj, proj)] = row.T

    def columns(source):
        blocks = pl.ds(source * nb, nb)
        row = q_rows[lax.rem(e - source + ex, ex), 0:1, :]
        col = jnp.broadcast_to(row, (LANES, rows_e)).T.reshape(nb, rows_p, LANES)
        q_col[blocks] = col
        wq_col[blocks] = wq_col[blocks] * col

    columns(e)
    wait_for(q_rows.at[pl.ds(1, 1)], n_recv.at[0])
    columns(sibling)
    v_own[...] = jnp.zeros_like(v_own)

    def finish(c):
        rows = rows_of(c)
        wait_for(rs_buf.at[:, rows], rs_recv.at[c])
        tot = part[z, x, rows, :]
        for j in range(half - 1):
            tot = tot + rs_buf[j, rows, :]
        scaled = float(cols * proj) ** 0.5 * tot * q_col[p, rows, 0:1] * t_scale[0:1, :]
        scores_ref[rows, :] = scaled.astype(jnp.bfloat16)

    def pass_on(i):
        s, c = i // chunks, lax.rem(i, chunks)
        chip = lax.rem(y - s + chips, chips)
        pairs = pl.ds(chip * nb, nb)
        wait_for(pair_buf.at[pairs, rows_of(c)], pair_recv.at[s, c])
        part[pairs, x, rows_of(c), :] = part[pairs, x, rows_of(c), :] + pair_buf[pairs, rows_of(c), :]
        for b in range(nb):
            to = chip * nb + b

            @pl.when(to != z)
            def _():
                pltpu.make_async_remote_copy(
                    src_ref=part.at[to, x, rows_of(c)],
                    dst_ref=rs_buf.at[lax.rem(to - z + half, half) - 1, rows_of(c)],
                    send_sem=rs_send.at[0],
                    recv_sem=rs_recv.at[c],
                    device_id={"proj": 2 * to + x},
                    device_id_type=MESH,
                ).start()

    prompt = chips * chunks - min(chunks, PROMPT)

    def step(i, carry):
        s, c = i // chunks, lax.rem(i, chunks)
        chip = lax.rem(y - s + chips, chips)

        @pl.when(i == chunks)
        def _():
            wait_for(q_rows.at[pl.ds(1, ex - 2)], n_recv.at[1])
            for d in range(1, chips):
                for k in range(2):
                    columns(lax.rem(y + d, chips) * 2 + k)

        @pl.when(s > 0)
        def _():
            got = qbuf.at[pl.ds((chip * 2 + core) * nb, nb), rows_of(c)]
            wait_for(got, y_recv.at[s - 1, c])
            sib_copy(s, c, False).start()

        wait_for(qbuf.at[pl.ds((chip * 2 + 1 - core) * nb, nb), rows_of(c)], sib_recv.at[s, c])
        blocks = pl.ds(chip * group, group)
        pairs = pl.ds(chip * nb, nb)
        depth = min(cols, 2048)
        acc = jnp.zeros((group * SLAB, n), jnp.float32)
        for k in range(0, cols, depth):
            q = qbuf[blocks, rows_of(c), k : k + depth].reshape(group * SLAB, depth)
            acc = acc + lax.dot_general(
                q, tbuf[:, k : k + depth], (((1,), (1,)), ((), ())), preferred_element_type=jnp.float32
            )
        part[pairs, :, rows_of(c), :] = acc.reshape(nb, 2, SLAB, n)
        pltpu.make_async_remote_copy(
            src_ref=part.at[pairs, 1 - x, rows_of(c)],
            dst_ref=pair_buf.at[pairs, rows_of(c)],
            send_sem=pair_send.at[s],
            recv_sem=pair_recv.at[s, c],
            device_id={"proj": partner},
            device_id_type=MESH,
        ).start()
        weighted = acc * wq_col[blocks, rows_of(c), 0:1].reshape(group * SLAB, 1)
        v_own[...] = v_own[...] + jnp.sum(weighted.reshape(group * SLAB // 8, 8, n), axis=0)

        @pl.when(i == chips * chunks - 1)
        def _():
            to_all(v_own, lambda d: v_buf.at[d - 1], v_send, v_recv)

        @pl.when((i > 0) & (i <= prompt))
        def _():
            pass_on(i - 1)

        @pl.when(i >= prompt)
        def _():
            pass_on(i)

        @pl.when(i > chunks * chips - chunks + 1)
        def _():
            finish(c - 2)

        return carry

    lax.fori_loop(0, chips * chunks, step, 0)
    wait_for(v_buf, v_recv.at[0])
    tot = v_own[...]
    for j in range(proj - 1):
        tot = tot + v_buf[j]
    tot = jnp.sum(tot, axis=0, keepdims=True) * t_scale[0:1, :]
    infl_ref[...] = tot * (float(cols * proj) ** 0.5 * (proj * rows_p) ** (-0.5))
    for c in range(max(chunks - 2, 0), chunks):
        finish(jnp.int32(c))

    for s in range(chips):
        wait_for(q_hbm, sib_send.at[s])
        wait_for(pair_buf.at[pl.ds(0, nb)], pair_send.at[s])
    for d in range(chips - 1):
        wait_for(q_hbm, y_send.at[d])
    wait_for(rs_buf, rs_send.at[0])
    wait_for(m_buf, m_send.at[0])
    wait_for(w_buf.at[pl.ds(1, proj - 1)], w_send.at[0])
    wait_for(q_rows.at[pl.ds(1, ex - 1)], n_send.at[0])
    wait_for(v_buf, v_send.at[0])


def body(ex, proj, queries, train_grads, query_weight):
    rows, cols = queries.shape
    n = train_grads.shape[0]
    rows_p = query_weight.shape[0]
    nb = rows // rows_p
    chips, chunks = ex // 2, rows_p // SLAB
    half = proj // 2
    f32, bf16 = jnp.float32, jnp.bfloat16
    vmem = pl.BlockSpec(memory_space=pltpu.VMEM)
    anywhere = pl.BlockSpec(memory_space=pl.ANY)
    dma = pltpu.SemaphoreType.DMA
    scores, influence = pl.pallas_call(
        functools.partial(kernel, ex, proj),
        out_shape=(jax.ShapeDtypeStruct((rows_p, n), bf16), jax.ShapeDtypeStruct((1, n), f32)),
        in_specs=[anywhere, anywhere, vmem],
        out_specs=(vmem, vmem),
        scratch_shapes=[
            pltpu.VMEM((proj, rows_p, cols), bf16),
            pltpu.VMEM((n, cols), bf16),
            pltpu.VMEM((half, 2, rows_p, n), f32),
            pltpu.VMEM((half, rows_p, n), f32),
            pltpu.VMEM((half - 1, rows_p, n), f32),
            pltpu.VMEM((n + rows, LANES), f32),
            pltpu.VMEM((8, n + rows), f32),
            pltpu.VMEM((proj - 1, 8, n + rows), f32),
            pltpu.VMEM((proj, 8, rows_p), f32),
            pltpu.VMEM((ex, 8, rows), f32),
            pltpu.VMEM((proj, rows_p, LANES), f32),
            pltpu.VMEM((proj, rows_p, LANES), f32),
            pltpu.VMEM((8, n), f32),
            pltpu.VMEM((8, n), f32),
            pltpu.VMEM((proj - 1, 8, n), f32),
            dma((2,)),
            dma((chips - 1,)),
            dma((chips - 1, chunks)),
            dma((chips,)),
            dma((chips, chunks)),
            dma((chips,)),
            dma((chips, chunks)),
            dma((1,)),
            dma((chunks,)),
            dma((1,)),
            dma((1,)),
            dma((1,)),
            dma((1,)),
            dma((1,)),
            dma((2,)),
            dma((1,)),
            dma((1,)),
        ],
        compiler_params=pltpu.CompilerParams(
            collective_id=0, has_side_effects=True, vmem_limit_bytes=56 * 2**20
        ),
        name="scores_ring",
    )(queries.reshape(nb, rows_p, cols), train_grads, query_weight.reshape(1, rows_p))
    return scores, influence.reshape(n)


def solution(mesh):
    return jax.shard_map(
        functools.partial(body, mesh.shape["ex"], mesh.shape["proj"]),
        mesh=mesh,
        in_specs=(P("ex", "proj"), P("ex", "proj"), P("proj")),
        out_specs=(P("proj", "ex"), P("ex")),
        check_vma=False,
    )
```

```python
import functools

import jax
import jax.numpy as jnp
from jax import lax
from jax.experimental import pallas as pl
from jax.experimental.pallas import tpu as pltpu
from jax.sharding import PartitionSpec as P

MESH = pl.DeviceIdType.MESH
SLAB = 16
FIRST = 2
LANES = 128
DEPTH = 2048
PROMPT = 3


def kernel(
    ex, proj, q_hbm, t_hbm, w_ref,
    scores_ref, infl_ref,
    qbuf, tbuf, part, pair_buf, rs_buf, lanes, m_own, m_buf, w_buf, q_rows, q_col, wq_col, t_scale, v_own, v_buf,
    load_sem, y_send, y_recv, sib_send, sib_recv, pair_send, pair_recv, rs_send, rs_recv,
    m_send, m_recv, w_send, w_recv, n_send, n_recv, v_send, v_recv,
):
    nb, rows_p, cols = q_hbm.shape
    n = t_hbm.shape[0]
    rows_e = nb * rows_p
    chips = ex // 2
    half = proj // 2
    chunks = rows_p // SLAB
    depth = min(cols, DEPTH)
    pieces = cols // depth
    group = 2 * nb
    e = lax.axis_index("ex")
    p = lax.axis_index("proj")
    y, core = e // 2, e % 2
    z, x = p // 2, p % 2
    sibling = e + 1 - 2 * core
    partner = p + 1 - 2 * x

    load_t = pltpu.make_async_copy(t_hbm, tbuf, load_sem.at[0])
    load_q = pltpu.make_async_copy(q_hbm, qbuf.at[pl.ds(e * nb, nb)], load_sem.at[1])

    barrier = pltpu.get_barrier_semaphore()
    for d in range(1, ex):
        pl.semaphore_signal(barrier, inc=1, device_id={"ex": lax.rem(e + d, ex)}, device_id_type=MESH)
    for d in range(1, proj):
        pl.semaphore_signal(barrier, inc=1, device_id={"proj": lax.rem(p + d, proj)}, device_id_type=MESH)
    load_q.start()
    load_t.start()
    pl.semaphore_wait(barrier, ex + proj - 2)

    def rows_of(c):
        return pl.ds(pl.multiple_of(c * SLAB, SLAB), SLAB)

    def send_y(i):
        d, c = i // chunks, lax.rem(i, chunks)
        for j in range(pieces):
            pltpu.make_async_remote_copy(
                src_ref=q_hbm.at[:, rows_of(c), pl.ds(j * depth, depth)],
                dst_ref=qbuf.at[pl.ds(e * nb, nb), rows_of(c), pl.ds(j * depth, depth)],
                send_sem=y_send.at[d],
                recv_sem=y_recv.at[d, c, j],
                device_id={"ex": lax.rem(y + d + 1, chips) * 2 + core},
                device_id_type=MESH,
            ).start()

    def sib_copy(s, c, j, own):
        at = (lax.rem(y - s + chips, chips) * 2 + core) * nb
        dst = qbuf.at[pl.ds(at, nb), rows_of(c), pl.ds(j * depth, depth)]
        return pltpu.make_async_remote_copy(
            src_ref=q_hbm.at[:, rows_of(c), pl.ds(j * depth, depth)] if own else dst,
            dst_ref=dst,
            send_sem=sib_send.at[s],
            recv_sem=sib_recv.at[s, c, j],
            device_id={"ex": sibling},
            device_id_type=MESH,
        )

    total = (chips - 1) * chunks
    for i in range(min(FIRST, total)):
        send_y(jnp.int32(i))

    def to_all(src, slot, send, recv):
        for d in range(1, proj):
            pltpu.make_async_remote_copy(
                src_ref=src,
                dst_ref=slot(d),
                send_sem=send.at[0],
                recv_sem=recv.at[0],
                device_id={"proj": lax.rem(p + d, proj)},
                device_id_type=MESH,
            ).start()

    def wait_for(ref, sem):
        pltpu.make_async_copy(ref, ref, sem).wait()

    w_buf[0] = jnp.broadcast_to(w_ref[...], (8, rows_p))
    to_all(w_buf.at[0], lambda d: w_buf.at[d], w_send, w_recv)
    for c in range(chunks):
        for j in range(pieces):
            sib_copy(0, c, j, True).start()

    def norms(count, at, load):
        def one(g, carry):
            acc = jnp.zeros((SLAB, LANES), jnp.float32)
            for k in range(0, cols, LANES):
                v = load(g, k).astype(jnp.float32)
                acc = acc + v * v
            lanes[pl.ds(pl.multiple_of(at + g * SLAB, SLAB), SLAB), :] = acc
            return carry

        lax.fori_loop(0, count // SLAB, one, 0)

    load_q.wait()
    norms(rows_e, n, lambda g, k: qbuf[e * nb + g // chunks, rows_of(lax.rem(g, chunks)), k : k + LANES])
    load_t.wait()
    norms(n, 0, lambda g, k: tbuf[rows_of(g), k : k + LANES])
    m_own[...] = jnp.sum(lanes[...].T.reshape(LANES // 8, 8, n + rows_e), axis=0)
    to_all(m_own, lambda d: m_buf.at[d - 1], m_send, m_recv)
    wait_for(m_buf, m_recv.at[0])
    tot = m_own[...]
    for j in range(proj - 1):
        tot = tot + m_buf[j]
    tot = jnp.broadcast_to(jnp.sum(tot, axis=0, keepdims=True), tot.shape)
    scale = lax.rsqrt(tot + 1e-06)
    t_scale[...] = scale[:, :n]
    q_rows[0] = scale[:, n:]
    for d in range(1, ex):
        pltpu.make_async_remote_copy(
            src_ref=q_rows.at[0],
            dst_ref=q_rows.at[d],
            send_sem=n_send.at[0],
            recv_sem=n_recv.at[jnp.where(lax.rem(e + d, ex) == sibling, 0, 1)],
            device_id={"ex": lax.rem(e + d, ex)},
            device_id_type=MESH,
        ).start()
    for i in range(min(FIRST, total), total):
        send_y(jnp.int32(i))
    wait_for(w_buf.at[pl.ds(1, proj - 1)], w_recv.at[0])
    for d in range(proj):
        row = jnp.broadcast_to(w_buf[d, 0:1, :], (LANES, rows_p))
        wq_col[lax.rem(p - d + proj, proj)] = row.T

    def columns(source):
        blocks = pl.ds(source * nb, nb)
        row = q_rows[lax.rem(e - source + ex, ex), 0:1, :]
        col = jnp.broadcast_to(row, (LANES, rows_e)).T.reshape(nb, rows_p, LANES)
        q_col[blocks] = col
        wq_col[blocks] = wq_col[blocks] * col

    columns(e)
    wait_for(q_rows.at[pl.ds(1, 1)], n_recv.at[0])
    columns(sibling)
    v_own[...] = jnp.zeros_like(v_own)

    def finish(c):
        rows = rows_of(c)
        wait_for(rs_buf.at[:, rows], rs_recv.at[c])
        tot = part[z, x, rows, :]
        for j in range(half - 1):
            tot = tot + rs_buf[j, rows, :]
        scaled = float(cols * proj) ** 0.5 * tot * q_col[p, rows, 0:1] * t_scale[0:1, :]
        scores_ref[rows, :] = scaled.astype(jnp.bfloat16)

    def pass_on(i):
        s, c = i // chunks, lax.rem(i, chunks)
        chip = lax.rem(y - s + chips, chips)
        pairs = pl.ds(chip * nb, nb)
        wait_for(pair_buf.at[pairs, rows_of(c)], pair_recv.at[s, c])
        part[pairs, x, rows_of(c), :] = part[pairs, x, rows_of(c), :] + pair_buf[pairs, rows_of(c), :]
        for b in range(nb):
            to = chip * nb + b

            @pl.when(to != z)
            def _():
                pltpu.make_async_remote_copy(
                    src_ref=part.at[to, x, rows_of(c)],
                    dst_ref=rs_buf.at[lax.rem(to - z + half, half) - 1, rows_of(c)],
                    send_sem=rs_send.at[0],
                    recv_sem=rs_recv.at[c],
                    device_id={"proj": 2 * to + x},
                    device_id_type=MESH,
                ).start()

    prompt = chips * chunks - min(chunks, PROMPT)

    def step(i, carry):
        s, c = i // chunks, lax.rem(i, chunks)
        chip = lax.rem(y - s + chips, chips)

        @pl.when(i == chunks)
        def _():
            wait_for(q_rows.at[pl.ds(1, ex - 2)], n_recv.at[1])
            for d in range(1, chips):
                for k in range(2):
                    columns(lax.rem(y + d, chips) * 2 + k)

        def take(j):
            @pl.when(s > 0)
            def _():
                got = qbuf.at[pl.ds((chip * 2 + core) * nb, nb), rows_of(c), pl.ds(j * depth, depth)]
                wait_for(got, y_recv.at[s - 1, c, j])
                sib_copy(s, c, j, False).start()

        blocks = pl.ds(chip * group, group)
        pairs = pl.ds(chip * nb, nb)
        others = pl.ds((chip * 2 + 1 - core) * nb, nb)
        acc = jnp.zeros((group * SLAB, n), jnp.float32)
        take(0)
        for j in range(pieces):
            if j + 1 < pieces:
                take(j + 1)
            at = pl.ds(j * depth, depth)
            wait_for(qbuf.at[others, rows_of(c), at], sib_recv.at[s, c, j])
            q = qbuf[blocks, rows_of(c), at].reshape(group * SLAB, depth)
            acc = acc + lax.dot_general(
                q, tbuf[:, at], (((1,), (1,)), ((), ())), preferred_element_type=jnp.float32
            )
        part[pairs, :, rows_of(c), :] = acc.reshape(nb, 2, SLAB, n)
        pltpu.make_async_remote_copy(
            src_ref=part.at[pairs, 1 - x, rows_of(c)],
            dst_ref=pair_buf.at[pairs, rows_of(c)],
            send_sem=pair_send.at[s],
            recv_sem=pair_recv.at[s, c],
            device_id={"proj": partner},
            device_id_type=MESH,
        ).start()
        weighted = acc * wq_col[blocks, rows_of(c), 0:1].reshape(group * SLAB, 1)
        v_own[...] = v_own[...] + jnp.sum(weighted.reshape(group * SLAB // 8, 8, n), axis=0)

        @pl.when(i == chips * chunks - 1)
        def _():
            to_all(v_own, lambda d: v_buf.at[d - 1], v_send, v_recv)

        @pl.when((i > 0) & (i <= prompt))
        def _():
            pass_on(i - 1)

        @pl.when(i >= prompt)
        def _():
            pass_on(i)

        @pl.when(i > chunks * chips - chunks + 1)
        def _():
            finish(c - 2)

        return carry

    lax.fori_loop(0, chips * chunks, step, 0)
    wait_for(v_buf, v_recv.at[0])
    tot = v_own[...]
    for j in range(proj - 1):
        tot = tot + v_buf[j]
    tot = jnp.sum(tot, axis=0, keepdims=True) * t_scale[0:1, :]
    infl_ref[...] = tot * (float(cols * proj) ** 0.5 * (proj * rows_p) ** (-0.5))
    for c in range(max(chunks - 2, 0), chunks):
        finish(jnp.int32(c))

    for s in range(chips):
        wait_for(q_hbm, sib_send.at[s])
        wait_for(pair_buf.at[pl.ds(0, nb)], pair_send.at[s])
    for d in range(chips - 1):
        wait_for(q_hbm, y_send.at[d])
    wait_for(rs_buf, rs_send.at[0])
    wait_for(m_buf, m_send.at[0])
    wait_for(w_buf.at[pl.ds(1, proj - 1)], w_send.at[0])
    wait_for(q_rows.at[pl.ds(1, ex - 1)], n_send.at[0])
    wait_for(v_buf, v_send.at[0])


def settle(scores_ref, infl_ref, scores_out, infl_out):
    scores_out[...] = scores_ref[...]
    infl_out[...] = infl_ref[0, :]


def body(ex, proj, queries, train_grads, query_weight):
    rows, cols = queries.shape
    n = train_grads.shape[0]
    rows_p = query_weight.shape[0]
    nb = rows // rows_p
    chips, chunks = ex // 2, rows_p // SLAB
    half = proj // 2
    f32, bf16 = jnp.float32, jnp.bfloat16
    vmem = pl.BlockSpec(memory_space=pltpu.VMEM)
    anywhere = pl.BlockSpec(memory_space=pl.ANY)
    dma = pltpu.SemaphoreType.DMA
    scores, influence = pl.pallas_call(
        functools.partial(kernel, ex, proj),
        out_shape=(jax.ShapeDtypeStruct((rows_p, n), bf16), jax.ShapeDtypeStruct((1, n), f32)),
        in_specs=[anywhere, anywhere, vmem],
        out_specs=(vmem, vmem),
        scratch_shapes=[
            pltpu.VMEM((proj, rows_p, cols), bf16),
            pltpu.VMEM((n, cols), bf16),
            pltpu.VMEM((half, 2, rows_p, n), f32),
            pltpu.VMEM((half, rows_p, n), f32),
            pltpu.VMEM((half - 1, rows_p, n), f32),
            pltpu.VMEM((n + rows, LANES), f32),
            pltpu.VMEM((8, n + rows), f32),
            pltpu.VMEM((proj - 1, 8, n + rows), f32),
            pltpu.VMEM((proj, 8, rows_p), f32),
            pltpu.VMEM((ex, 8, rows), f32),
            pltpu.VMEM((proj, rows_p, LANES), f32),
            pltpu.VMEM((proj, rows_p, LANES), f32),
            pltpu.VMEM((8, n), f32),
            pltpu.VMEM((8, n), f32),
            pltpu.VMEM((proj - 1, 8, n), f32),
            dma((2,)),
            dma((chips - 1,)),
            dma((chips - 1, chunks, max(cols // DEPTH, 1))),
            dma((chips,)),
            dma((chips, chunks, max(cols // DEPTH, 1))),
            dma((chips,)),
            dma((chips, chunks)),
            dma((1,)),
            dma((chunks,)),
            dma((1,)),
            dma((1,)),
            dma((1,)),
            dma((1,)),
            dma((1,)),
            dma((2,)),
            dma((1,)),
            dma((1,)),
        ],
        compiler_params=pltpu.CompilerParams(
            collective_id=0, has_side_effects=True, vmem_limit_bytes=56 * 2**20
        ),
        name="scores_ring",
    )(queries.reshape(nb, rows_p, cols), train_grads, query_weight.reshape(1, rows_p))
    return pl.pallas_call(
        settle,
        out_shape=(jax.ShapeDtypeStruct((rows_p, n), bf16), jax.ShapeDtypeStruct((n,), f32)),
        in_specs=[vmem, vmem],
        out_specs=(vmem, vmem),
        name="settle",
    )(scores, influence)


def solution(mesh):
    return jax.shard_map(
        functools.partial(body, mesh.shape["ex"], mesh.shape["proj"]),
        mesh=mesh,
        in_specs=(P("ex", "proj"), P("ex", "proj"), P("proj")),
        out_specs=(P("proj", "ex"), P("ex")),
        check_vma=False,
    )
```

```python
import functools

import jax
import jax.numpy as jnp
from jax import lax
from jax.experimental import pallas as pl
from jax.experimental.pallas import tpu as pltpu
from jax.sharding import PartitionSpec as P

MESH = pl.DeviceIdType.MESH
SLAB = 16
FIRST = 2
LANES = 128
DEPTH = 2048
PROMPT = 3


def kernel(
    ex, proj, q_hbm, t_hbm, w_ref,
    scores_ref, infl_ref,
    qbuf, tbuf, part, pair_buf, rs_buf, lanes, m_own, m_buf, w_buf, q_rows, q_col, wq_col, t_scale, v_own, v_row, v_buf,
    load_sem, y_send, y_recv, sib_send, sib_recv, pair_send, pair_recv, rs_send, rs_recv,
    m_send, m_recv, w_send, w_recv, n_send, n_recv, v_send, v_recv,
):
    nb, rows_p, cols = q_hbm.shape
    n = t_hbm.shape[0]
    rows_e = nb * rows_p
    chips = ex // 2
    half = proj // 2
    chunks = rows_p // SLAB
    depth = min(cols, DEPTH)
    pieces = cols // depth
    group = 2 * nb
    e = lax.axis_index("ex")
    p = lax.axis_index("proj")
    y, core = e // 2, e % 2
    z, x = p // 2, p % 2
    sibling = e + 1 - 2 * core
    partner = p + 1 - 2 * x

    load_t = pltpu.make_async_copy(t_hbm, tbuf, load_sem.at[0])
    load_q = pltpu.make_async_copy(q_hbm, qbuf.at[pl.ds(e * nb, nb)], load_sem.at[1])

    barrier = pltpu.get_barrier_semaphore()
    for d in range(1, ex):
        pl.semaphore_signal(barrier, inc=1, device_id={"ex": lax.rem(e + d, ex)}, device_id_type=MESH)
    for d in range(1, proj):
        pl.semaphore_signal(barrier, inc=1, device_id={"proj": lax.rem(p + d, proj)}, device_id_type=MESH)
    load_q.start()
    load_t.start()
    pl.semaphore_wait(barrier, ex + proj - 2)

    def rows_of(c):
        return pl.ds(pl.multiple_of(c * SLAB, SLAB), SLAB)

    def send_y(i):
        d, c = i // chunks, lax.rem(i, chunks)
        for j in range(pieces):
            pltpu.make_async_remote_copy(
                src_ref=q_hbm.at[:, rows_of(c), pl.ds(j * depth, depth)],
                dst_ref=qbuf.at[pl.ds(e * nb, nb), rows_of(c), pl.ds(j * depth, depth)],
                send_sem=y_send.at[d],
                recv_sem=y_recv.at[d, c, j],
                device_id={"ex": lax.rem(y + d + 1, chips) * 2 + core},
                device_id_type=MESH,
            ).start()

    def sib_copy(s, c, j, own):
        at = (lax.rem(y - s + chips, chips) * 2 + core) * nb
        dst = qbuf.at[pl.ds(at, nb), rows_of(c), pl.ds(j * depth, depth)]
        return pltpu.make_async_remote_copy(
            src_ref=q_hbm.at[:, rows_of(c), pl.ds(j * depth, depth)] if own else dst,
            dst_ref=dst,
            send_sem=sib_send.at[s],
            recv_sem=sib_recv.at[s, c, j],
            device_id={"ex": sibling},
            device_id_type=MESH,
        )

    total = (chips - 1) * chunks
    for i in range(min(FIRST, total)):
        send_y(jnp.int32(i))

    def to_all(src, slot, send, recv):
        for d in range(1, proj):
            pltpu.make_async_remote_copy(
                src_ref=src,
                dst_ref=slot(d),
                send_sem=send.at[0],
                recv_sem=recv.at[0],
                device_id={"proj": lax.rem(p + d, proj)},
                device_id_type=MESH,
            ).start()

    def wait_for(ref, sem):
        pltpu.make_async_copy(ref, ref, sem).wait()

    w_buf[0] = jnp.broadcast_to(w_ref[...], (8, rows_p))
    to_all(w_buf.at[0], lambda d: w_buf.at[d], w_send, w_recv)
    for c in range(chunks):
        for j in range(pieces):
            sib_copy(0, c, j, True).start()

    def norms(count, at, load):
        def one(g, carry):
            acc = jnp.zeros((SLAB, LANES), jnp.float32)
            for k in range(0, cols, LANES):
                v = load(g, k).astype(jnp.float32)
                acc = acc + v * v
            lanes[pl.ds(pl.multiple_of(at + g * SLAB, SLAB), SLAB), :] = acc
            return carry

        lax.fori_loop(0, count // SLAB, one, 0)

    load_q.wait()
    norms(rows_e, n, lambda g, k: qbuf[e * nb + g // chunks, rows_of(lax.rem(g, chunks)), k : k + LANES])
    load_t.wait()
    norms(n, 0, lambda g, k: tbuf[rows_of(g), k : k + LANES])
    m_own[...] = jnp.sum(lanes[...].T.reshape(LANES // 8, 8, n + rows_e), axis=0)
    to_all(m_own, lambda d: m_buf.at[d - 1], m_send, m_recv)
    wait_for(m_buf, m_recv.at[0])
    tot = m_own[...]
    for j in range(proj - 1):
        tot = tot + m_buf[j]
    tot = jnp.broadcast_to(jnp.sum(tot, axis=0, keepdims=True), tot.shape)
    scale = lax.rsqrt(tot + 1e-06)
    t_scale[...] = scale[:, :n]
    q_rows[0] = scale[:, n:]
    for d in range(1, ex):
        pltpu.make_async_remote_copy(
            src_ref=q_rows.at[0],
            dst_ref=q_rows.at[d],
            send_sem=n_send.at[0],
            recv_sem=n_recv.at[jnp.where(lax.rem(e + d, ex) == sibling, 0, 1)],
            device_id={"ex": lax.rem(e + d, ex)},
            device_id_type=MESH,
        ).start()
    for i in range(min(FIRST, total), total):
        send_y(jnp.int32(i))
    wait_for(w_buf.at[pl.ds(1, proj - 1)], w_recv.at[0])
    for d in range(proj):
        row = jnp.broadcast_to(w_buf[d, 0:1, :], (LANES, rows_p))
        wq_col[lax.rem(p - d + proj, proj)] = row.T

    def columns(source):
        blocks = pl.ds(source * nb, nb)
        row = q_rows[lax.rem(e - source + ex, ex), 0:1, :]
        col = jnp.broadcast_to(row, (LANES, rows_e)).T.reshape(nb, rows_p, LANES)
        q_col[blocks] = col
        wq_col[blocks] = wq_col[blocks] * col

    columns(e)
    wait_for(q_rows.at[pl.ds(1, 1)], n_recv.at[0])
    columns(sibling)
    v_own[...] = jnp.zeros_like(v_own)

    def finish(c):
        rows = rows_of(c)
        wait_for(rs_buf.at[:, rows], rs_recv.at[c])
        tot = part[z, x, rows, :]
        for j in range(half - 1):
            tot = tot + rs_buf[j, rows, :]
        scaled = float(cols * proj) ** 0.5 * tot * q_col[p, rows, 0:1] * t_scale[0:1, :]
        scores_ref[rows, :] = scaled.astype(jnp.bfloat16)

    def pass_on(i):
        s, c = i // chunks, lax.rem(i, chunks)
        chip = lax.rem(y - s + chips, chips)
        pairs = pl.ds(chip * nb, nb)
        wait_for(pair_buf.at[pairs, rows_of(c)], pair_recv.at[s, c])
        part[pairs, x, rows_of(c), :] = part[pairs, x, rows_of(c), :] + pair_buf[pairs, rows_of(c), :]
        for b in range(nb):
            to = chip * nb + b

            @pl.when(to != z)
            def _():
                pltpu.make_async_remote_copy(
                    src_ref=part.at[to, x, rows_of(c)],
                    dst_ref=rs_buf.at[lax.rem(to - z + half, half) - 1, rows_of(c)],
                    send_sem=rs_send.at[0],
                    recv_sem=rs_recv.at[c],
                    device_id={"proj": 2 * to + x},
                    device_id_type=MESH,
                ).start()

    prompt = chips * chunks - min(chunks, PROMPT)

    def step(i, carry):
        s, c = i // chunks, lax.rem(i, chunks)
        chip = lax.rem(y - s + chips, chips)

        @pl.when(i == chunks)
        def _():
            wait_for(q_rows.at[pl.ds(1, ex - 2)], n_recv.at[1])
            for d in range(1, chips):
                for k in range(2):
                    columns(lax.rem(y + d, chips) * 2 + k)

        def take(j):
            @pl.when(s > 0)
            def _():
                got = qbuf.at[pl.ds((chip * 2 + core) * nb, nb), rows_of(c), pl.ds(j * depth, depth)]
                wait_for(got, y_recv.at[s - 1, c, j])
                sib_copy(s, c, j, False).start()

        blocks = pl.ds(chip * group, group)
        pairs = pl.ds(chip * nb, nb)
        others = pl.ds((chip * 2 + 1 - core) * nb, nb)
        acc = jnp.zeros((group * SLAB, n), jnp.float32)
        take(0)
        for j in range(pieces):
            if j + 1 < pieces:
                take(j + 1)
            at = pl.ds(j * depth, depth)
            wait_for(qbuf.at[others, rows_of(c), at], sib_recv.at[s, c, j])
            q = qbuf[blocks, rows_of(c), at].reshape(group * SLAB, depth)
            acc = acc + lax.dot_general(
                q, tbuf[:, at], (((1,), (1,)), ((), ())), preferred_element_type=jnp.float32
            )
        part[pairs, :, rows_of(c), :] = acc.reshape(nb, 2, SLAB, n)
        pltpu.make_async_remote_copy(
            src_ref=part.at[pairs, 1 - x, rows_of(c)],
            dst_ref=pair_buf.at[pairs, rows_of(c)],
            send_sem=pair_send.at[s],
            recv_sem=pair_recv.at[s, c],
            device_id={"proj": partner},
            device_id_type=MESH,
        ).start()
        weighted = acc * wq_col[blocks, rows_of(c), 0:1].reshape(group * SLAB, 1)
        v_own[...] = v_own[...] + jnp.sum(weighted.reshape(group * SLAB // 8, 8, n), axis=0)

        @pl.when(i == chips * chunks - 1)
        def _():
            v_row[...] = jnp.sum(v_own[...], axis=0, keepdims=True)
            to_all(v_row, lambda d: v_buf.at[d - 1], v_send, v_recv)

        @pl.when((i > 0) & (i <= prompt))
        def _():
            pass_on(i - 1)

        @pl.when(i >= prompt)
        def _():
            pass_on(i)

        @pl.when(i > chunks * chips - chunks + 1)
        def _():
            finish(c - 2)

        return carry

    lax.fori_loop(0, chips * chunks, step, 0)
    wait_for(v_buf, v_recv.at[0])
    tot = v_row[...]
    for j in range(proj - 1):
        tot = tot + v_buf[j]
    tot = tot * t_scale[0:1, :]
    infl_ref[...] = tot * (float(cols * proj) ** 0.5 * (proj * rows_p) ** (-0.5))
    for c in range(max(chunks - 2, 0), chunks):
        finish(jnp.int32(c))

    for s in range(chips):
        wait_for(q_hbm, sib_send.at[s])
        wait_for(pair_buf.at[pl.ds(0, nb)], pair_send.at[s])
    for d in range(chips - 1):
        wait_for(q_hbm, y_send.at[d])
    wait_for(rs_buf, rs_send.at[0])
    wait_for(m_buf, m_send.at[0])
    wait_for(w_buf.at[pl.ds(1, proj - 1)], w_send.at[0])
    wait_for(q_rows.at[pl.ds(1, ex - 1)], n_send.at[0])
    wait_for(v_buf, v_send.at[0])


def settle(scores_ref, infl_ref, scores_out, infl_out):
    scores_out[...] = scores_ref[...]
    infl_out[...] = infl_ref[0, :]


def body(ex, proj, queries, train_grads, query_weight):
    rows, cols = queries.shape
    n = train_grads.shape[0]
    rows_p = query_weight.shape[0]
    nb = rows // rows_p
    chips, chunks = ex // 2, rows_p // SLAB
    half = proj // 2
    f32, bf16 = jnp.float32, jnp.bfloat16
    vmem = pl.BlockSpec(memory_space=pltpu.VMEM)
    anywhere = pl.BlockSpec(memory_space=pl.ANY)
    dma = pltpu.SemaphoreType.DMA
    scores, influence = pl.pallas_call(
        functools.partial(kernel, ex, proj),
        out_shape=(jax.ShapeDtypeStruct((rows_p, n), bf16), jax.ShapeDtypeStruct((1, n), f32)),
        in_specs=[anywhere, anywhere, vmem],
        out_specs=(vmem, vmem),
        scratch_shapes=[
            pltpu.VMEM((proj, rows_p, cols), bf16),
            pltpu.VMEM((n, cols), bf16),
            pltpu.VMEM((half, 2, rows_p, n), f32),
            pltpu.VMEM((half, rows_p, n), f32),
            pltpu.VMEM((half - 1, rows_p, n), f32),
            pltpu.VMEM((n + rows, LANES), f32),
            pltpu.VMEM((8, n + rows), f32),
            pltpu.VMEM((proj - 1, 8, n + rows), f32),
            pltpu.VMEM((proj, 8, rows_p), f32),
            pltpu.VMEM((ex, 8, rows), f32),
            pltpu.VMEM((proj, rows_p, LANES), f32),
            pltpu.VMEM((proj, rows_p, LANES), f32),
            pltpu.VMEM((8, n), f32),
            pltpu.VMEM((8, n), f32),
            pltpu.VMEM((1, n), f32),
            pltpu.VMEM((proj - 1, 1, n), f32),
            dma((2,)),
            dma((chips - 1,)),
            dma((chips - 1, chunks, max(cols // DEPTH, 1))),
            dma((chips,)),
            dma((chips, chunks, max(cols // DEPTH, 1))),
            dma((chips,)),
            dma((chips, chunks)),
            dma((1,)),
            dma((chunks,)),
            dma((1,)),
            dma((1,)),
            dma((1,)),
            dma((1,)),
            dma((1,)),
            dma((2,)),
            dma((1,)),
            dma((1,)),
        ],
        compiler_params=pltpu.CompilerParams(
            collective_id=0, has_side_effects=True, vmem_limit_bytes=56 * 2**20
        ),
        name="scores_ring",
    )(queries.reshape(nb, rows_p, cols), train_grads, query_weight.reshape(1, rows_p))
    return pl.pallas_call(
        settle,
        out_shape=(jax.ShapeDtypeStruct((rows_p, n), bf16), jax.ShapeDtypeStruct((n,), f32)),
        in_specs=[vmem, vmem],
        out_specs=(vmem, vmem),
        name="settle",
    )(scores, influence)


def solution(mesh):
    return jax.shard_map(
        functools.partial(body, mesh.shape["ex"], mesh.shape["proj"]),
        mesh=mesh,
        in_specs=(P("ex", "proj"), P("ex", "proj"), P("proj")),
        out_specs=(P("proj", "ex"), P("ex")),
        check_vma=False,
    )
```
